128 devices in a mesh: row: 16 (over x_lo, z, core), col: 8 (over x_hi, y).
Axes of the slice: x: 4 (x_hi: 2, x_lo: 2; x = x_hi * 2 + x_lo), y: 4, z: 4, core: 2. Of those that a mesh axis runs over, the one named last changes fastest.
Arguments:
- matrix: bfloat16 [24576, 24576], P('row', 'col'), may hold values from -8 to 8, as said below
- panels: bfloat16 [2, 24576, 128], P(None, 'row'), may hold values from -1 to 1
Outputs:
- updated: bfloat16 [24576, 24576], P('row', 'col')
The draws below stay inside these ranges and needn't reach their ends.
Inputs may be any that keep to these rules, and one draw needn't show every extreme that they name: matrix is exactly symmetric.
All inputs are finite; a program needn't handle non-finite values.
Results may differ from the reference program's by a relative error of at most 0.015.
Values may be sent and summed in bfloat16 or wider, within the bound.
A program may use at most 128 MiB of HBM per device.

```python
import jax
import jax.numpy as jnp
from jax import lax

B = 128
PANELS = 2
N = 24576


def draw_matrix(key, part):
    values = jnp.clip(jax.random.normal(key, (N, N), jnp.float32), -5.0, 5.0)
    return ((values + values.T) * 0.7071).astype(jnp.bfloat16)


def draw_panels(key, part):
    values = jnp.clip(jax.random.normal(jax.random.fold_in(key, 7), (PANELS, N, B), jnp.float32), -6.0, 6.0)
    return (values * (B * N) ** (-0.25)).astype(jnp.bfloat16)


def setup_inputs(seed: int = 0) -> dict:
    streams_of = jax.random.split(jax.random.key(seed), 3)
    return {
        "matrix": draw_matrix(jax.random.fold_in(streams_of[2], 71), 0),
        "panels": draw_panels(jax.random.fold_in(streams_of[2], 71), 0),
    }


def reference(matrix, panels):
    current = matrix
    for panel in range(PANELS):
        panel_v = panels[panel]
        product = jnp.dot(current, panel_v, preferred_element_type=jnp.float32)
        panel_f = panel_v.astype(jnp.float32)
        curvature = jnp.dot(panel_f.T, product, precision=lax.Precision.HIGHEST)
        w_panel = (product - 0.5 * jnp.dot(panel_f, curvature, precision=lax.Precision.HIGHEST)).astype(jnp.bfloat16)
        update = lax.dot_general(panel_v, w_panel, (((1,), (1,)), ((), ())), preferred_element_type=jnp.float32)
        update = update + lax.dot_general(w_panel, panel_v, (((1,), (1,)), ((), ())), preferred_element_type=jnp.float32)
        current = (current.astype(jnp.float32) - update).astype(jnp.bfloat16)
    return current
```

```python
import functools

import jax
import jax.numpy as jnp
from jax import lax
from jax.experimental import pallas as pl
from jax.experimental.pallas import tpu as pltpu
from jax.sharding import PartitionSpec as P

MESH = pl.DeviceIdType.MESH
F32 = jnp.float32
BF16 = jnp.bfloat16

ROWS = 1536
HALVES = 2
WIDE = 256
SUB = 4
SUBW = ROWS // SUB
PIECE = 32
CROWS = PIECE + 16
NN = (((1,), (0,)), ((), ()))
NT = (((1,), (1,)), ((), ()))
TN = (((0,), (0,)), ((), ()))


def dot(a, b, dims, precision=None):
    return lax.dot_general(a, b, dims, preferred_element_type=F32, precision=precision)


def exchange_kernel(
    a_ref, v_ref, x_ref, y_ref,
    a_buf, vt, q_send, q_own, sib_in, x_send, x_own, x_in, z_send, z_in, piece, vpiece,
    turned, prt, c_send, c_sib, c_half, c_col, c_row, c_full,
    a_sem, s_send, s_recv,
):
    row = lax.axis_index("row")
    col = lax.axis_index("col")
    core = row % 2
    big = row // 2
    z = big % 4
    xl = big // 4

    sibling = (big * 2 + 1 - core, col)

    def row_peer(j):
        other = (xl + j // 4) % 2 * 4 + (z + j % 4) % 4
        return other, (other * 2 + core, col)

    def col_peer(j):
        other = (col // 4 + j // 4) % 2 * 4 + (col % 4 + j % 4) % 4
        return other, (row, other)

    mirror = (col * 2 + core, big)
    on_diagonal = big == col

    used = [0]

    def copy(src, dst, to):
        i = used[0]
        used[0] += 1
        return pltpu.make_async_remote_copy(
            src_ref=src, dst_ref=dst, send_sem=s_send.at[i], recv_sem=s_recv.at[i],
            device_id=to, device_id_type=MESH,
        )

    loads = []
    for s in range(SUB):
        for h in range(HALVES):
            half = 1 - core if h == 0 else core
            start = pl.multiple_of(half * ROWS + s * SUBW, 128)
            loads.append(
                pltpu.make_async_copy(a_ref.at[:, pl.ds(start, SUBW)], a_buf.at[2 * s + h], a_sem.at[2 * s + h])
            )
    for load in loads:
        load.start()

    barrier = pltpu.get_barrier_semaphore()
    pl.semaphore_signal(barrier, inc=1, device_id=sibling, device_id_type=MESH)
    for j in range(1, 8):
        pl.semaphore_signal(barrier, inc=1, device_id=row_peer(j)[1], device_id_type=MESH)
        pl.semaphore_signal(barrier, inc=1, device_id=col_peer(j)[1], device_id_type=MESH)

    @pl.when(jnp.logical_not(on_diagonal))
    def _():
        pl.semaphore_signal(barrier, inc=1, device_id=mirror, device_id_type=MESH)

    vt[:128, :] = v_ref[0].T
    vt[128:, :] = v_ref[1].T

    @pl.when(on_diagonal)
    def _():
        pl.semaphore_wait(barrier, 15)

    @pl.when(jnp.logical_not(on_diagonal))
    def _():
        pl.semaphore_wait(barrier, 16)

    v_turn = copy(vt.at[pl.ds(pl.multiple_of(col * PIECE, PIECE), PIECE)], vpiece, mirror)

    @pl.when(jnp.logical_not(on_diagonal))
    def _():
        v_turn.start()

    @pl.when(on_diagonal)
    def _():
        vpiece[...] = vt[pl.ds(pl.multiple_of(col * PIECE, PIECE), PIECE), :]

    sib = []
    for s in range(SUB):
        loads[2 * s].wait()
        q_send[s] = dot(vt[...], a_buf[2 * s], NN).astype(BF16)
        sib.append(copy(q_send.at[s], sib_in.at[s], sibling))
        sib[s].start()
        loads[2 * s + 1].wait()
        q_own[s] = dot(vt[...], a_buf[2 * s + 1], NN)

    mine = pl.multiple_of(big * PIECE, PIECE)
    my_half = pl.multiple_of(core * ROWS, ROWS)
    @pl.when(jnp.logical_not(on_diagonal))
    def _():
        v_turn.wait()
    y_ref[pl.ds(WIDE + mine, PIECE), pl.ds(my_half, ROWS)] = vpiece[...]
    v_gather = []
    for j in range(1, 8):
        c = copy(vpiece, y_ref.at[pl.ds(WIDE + mine, PIECE), pl.ds(my_half, ROWS)], row_peer(j)[1])
        c.start()
        v_gather.append(c)

    other_x = ((1 - xl) * 4 + z) * 2 + core
    xs = []
    for s in range(SUB):
        sib[s].wait_recv()
        x_send[s] = (
            q_own[s, pl.ds(pl.multiple_of((1 - xl) * 128, 128), 128)]
            + sib_in[s, pl.ds(pl.multiple_of((1 - xl) * 128, 128), 128)].astype(F32)
        ).astype(BF16)
        xs.append(copy(x_send.at[s], x_in.at[s], (other_x, col)))
        xs[s].start()
        x_own[s] = q_own[s, pl.ds(pl.multiple_of(xl * 128, 128), 128)] + sib_in[
            s, pl.ds(pl.multiple_of(xl * 128, 128), 128)
        ].astype(F32)
    zs = []
    for s in range(SUB):
        xs[s].wait_recv()
        x_own[s] = x_own[s] + x_in[s].astype(F32)
        z_send[s] = x_own[s].astype(BF16)
        for j in range(1, 4):
            to = (z + j) % 4
            c = copy(
                z_send.at[s, pl.ds(pl.multiple_of(to * PIECE, PIECE), PIECE)],
                z_in.at[s, j - 1],
                ((xl * 4 + to) * 2 + core, col),
            )
            c.start()
            zs.append(c)
    for s in range(SUB):
        total = x_own[s, pl.ds(pl.multiple_of(z * PIECE, PIECE), PIECE)]
        for j in range(3):
            zs[3 * s + j].wait_recv()
            total = total + z_in[s, j].astype(F32)
        piece[:, s * SUBW:(s + 1) * SUBW] = total.astype(BF16)

    p_turn = copy(piece, turned, mirror)

    @pl.when(jnp.logical_not(on_diagonal))
    def _():
        p_turn.start()

    @pl.when(on_diagonal)
    def _():
        turned[...] = piece[...]

    p_gather = []
    for j in range(1, 8):
        c = copy(piece, y_ref.at[pl.ds(mine, PIECE), pl.ds(my_half, ROWS)], row_peer(j)[1])
        c.start()
        p_gather.append(c)
    y_ref[pl.ds(mine, PIECE), pl.ds(my_half, ROWS)] = piece[...]

    for c in v_gather:
        c.wait_recv()
    v_share = copy(
        y_ref.at[pl.ds(WIDE, WIDE), pl.ds(my_half, ROWS)],
        y_ref.at[pl.ds(WIDE, WIDE), pl.ds(my_half, ROWS)], sibling,
    )
    v_share.start()

    v_half = y_ref[pl.ds(WIDE, WIDE), pl.ds(my_half, ROWS)]
    c_send[:PIECE, :] = dot(piece[...], v_half, NT)
    c_send[PIECE:, :] = dot(
        y_ref[pl.ds(pl.multiple_of(WIDE + big * 16, 16), 16), pl.ds(my_half, ROWS)], v_half, NT
    )
    hrows = CROWS // 2
    c_pair = copy(c_send.at[pl.ds(pl.multiple_of((1 - core) * hrows, 8), hrows)], c_sib, sibling)
    c_pair.start()

    @pl.when(jnp.logical_not(on_diagonal))
    def _():
        p_turn.wait()
    mine_r = pl.multiple_of(col * PIECE, PIECE)
    prt[pl.ds(mine_r, PIECE), :] = turned[...]
    r_gather = []
    for j in range(1, 8):
        c = copy(turned, prt.at[pl.ds(mine_r, PIECE)], col_peer(j)[1])
        c.start()
        r_gather.append(c)

    c_pair.wait_recv()
    c_half[...] = c_send[pl.ds(pl.multiple_of(core * hrows, 8), hrows), :] + c_sib[...]
    cc = []
    for j in range(1, 8):
        c = copy(c_half, c_col.at[j - 1], col_peer(j)[1])
        c.start()
        cc.append(c)
    total = c_half[...]
    for j in range(7):
        cc[j].wait_recv()
        total = total + c_col[j]
    c_row[...] = total
    slot = big * 2 + core
    cr = []
    for j in range(1, 8):
        c = copy(c_row, c_full.at[slot], row_peer(j)[1])
        c.start()
        cr.append(c)
    c = copy(c_row, c_full.at[slot], sibling)
    c.start()
    cr.append(c)
    c_full[slot] = c_row[...]
    for c in cr:
        c.wait_recv()
    fwd = []
    for j in range(1, 8):
        other = row_peer(j)[0] * 2 + core
        c = copy(c_full.at[other], c_full.at[other], sibling)
        c.start()
        fwd.append(c)
    for c in fwd:
        c.wait_recv()

    crows = [jnp.concatenate([c_full[2 * i], c_full[2 * i + 1]], axis=0) for i in range(8)]
    cpv = jnp.concatenate([m[:PIECE] for m in crows], axis=0)
    g01 = jnp.concatenate([m[PIECE:, 128:] for m in crows], axis=0)
    hi = lax.Precision.HIGHEST
    c00 = cpv[:128, :128]
    c01 = cpv[:128, 128:]
    c11 = cpv[128:, 128:]
    d = c01 - dot(c00, g01, NN, hi)
    curv = c11 - dot(c01, g01, TN, hi) - dot(g01, d, TN, hi)
    t2 = -jnp.concatenate(
        [jnp.concatenate([c00, d], axis=1), jnp.concatenate([d.T, curv], axis=1)], axis=0
    )
    t2b = t2.astype(BF16)
    g01b = g01.astype(BF16)

    v0 = v_ref[0]
    v1 = v_ref[1]
    x_ref[:, :128] = (v0.astype(F32) - dot(v1, g01b, NT)).astype(BF16)
    x_ref[:, 128:256] = v1
    vt2 = dot(v0, t2b[:128], NN) + dot(v1, t2b[128:], NN)

    for c in p_gather:
        c.wait_recv()
    p_share = copy(
        y_ref.at[pl.ds(0, WIDE), pl.ds(my_half, ROWS)],
        y_ref.at[pl.ds(0, WIDE), pl.ds(my_half, ROWS)], sibling,
    )
    p_share.start()
    for c in r_gather:
        c.wait_recv()
    p0 = prt[:128, :].T
    p1 = prt[128:, :].T
    x_ref[:, 256:384] = (vt2[:, :128] + p0.astype(F32)).astype(BF16)
    x_ref[:, 384:] = (vt2[:, 128:] + p1.astype(F32) - dot(p0, g01b, NN)).astype(BF16)

    for c in sib + v_gather + xs + zs + p_gather + [c_pair] + r_gather + cc + cr + fwd:
        c.wait_send()
    v_share.wait()
    p_share.wait()


N_COPIES = 1 + SUB + 7 + SUB + 3 * SUB + 1 + 7 + 1 + 1 + 7 + 7 + 8 + 7 + 1


def exchange(matrix, panels):
    return pl.pallas_call(
        exchange_kernel,
        out_shape=(
            jax.ShapeDtypeStruct((ROWS, 2 * WIDE), BF16),
            jax.ShapeDtypeStruct((2 * WIDE, 2 * ROWS), BF16),
        ),
        in_specs=[pl.BlockSpec(memory_space=pl.ANY), pl.BlockSpec(memory_space=pltpu.VMEM)],
        out_specs=(pl.BlockSpec(memory_space=pltpu.VMEM), pl.BlockSpec(memory_space=pltpu.VMEM)),
        scratch_shapes=[
            pltpu.VMEM((2 * SUB, ROWS, SUBW), BF16),
            pltpu.VMEM((WIDE, ROWS), BF16),
            pltpu.VMEM((SUB, WIDE, SUBW), BF16),
            pltpu.VMEM((SUB, WIDE, SUBW), F32),
            pltpu.VMEM((SUB, WIDE, SUBW), BF16),
            pltpu.VMEM((SUB, 128, SUBW), BF16),
            pltpu.VMEM((SUB, 128, SUBW), F32),
            pltpu.VMEM((SUB, 128, SUBW), BF16),
            pltpu.VMEM((SUB, 128, SUBW), BF16),
            pltpu.VMEM((SUB, 3, PIECE, SUBW), BF16),
            pltpu.VMEM((PIECE, ROWS), BF16),
            pltpu.VMEM((PIECE, ROWS), BF16),
            pltpu.VMEM((PIECE, ROWS), BF16),
            pltpu.VMEM((WIDE, ROWS), BF16),
            pltpu.VMEM((CROWS, WIDE), F32),
            pltpu.VMEM((CROWS // 2, WIDE), F32),
            pltpu.VMEM((CROWS // 2, WIDE), F32),
            pltpu.VMEM((7, CROWS // 2, WIDE), F32),
            pltpu.VMEM((CROWS // 2, WIDE), F32),
            pltpu.VMEM((16, CROWS // 2, WIDE), F32),
            pltpu.SemaphoreType.DMA((2 * SUB,)),
            pltpu.SemaphoreType.DMA((N_COPIES,)),
            pltpu.SemaphoreType.DMA((N_COPIES,)),
        ],
        compiler_params=pltpu.CompilerParams(
            collective_id=0, has_side_effects=True, vmem_limit_bytes=48 * 2**20
        ),
        name="exchange",
    )(matrix, panels)


def update_kernel(a_ref, x_ref, y_ref, o_ref):
    o_ref[...] = (a_ref[...].astype(F32) - dot(x_ref[...], y_ref[...], NN)).astype(BF16)


def update(matrix, x, y):
    block = 256
    return pl.pallas_call(
        update_kernel,
        out_shape=jax.ShapeDtypeStruct(matrix.shape, BF16),
        grid=(matrix.shape[1] // block,),
        in_specs=[
            pl.BlockSpec((ROWS, block), lambda i: (0, i)),
            pl.BlockSpec((ROWS, 2 * WIDE), lambda i: (0, 0)),
            pl.BlockSpec((2 * WIDE, block), lambda i: (0, i)),
        ],
        out_specs=pl.BlockSpec((ROWS, block), lambda i: (0, i)),
        compiler_params=pltpu.CompilerParams(vmem_limit_bytes=48 * 2**20),
        name="update",
    )(matrix, x, y)


def per_device(matrix, panels):
    x, y = exchange(matrix, panels)
    return update(matrix, x, y)


def solution(mesh):
    return jax.shard_map(
        per_device,
        mesh=mesh,
        in_specs=(P("row", "col"), P(None, "row", None)),
        out_specs=P("row", "col"),
        check_vma=False,
    )
```

```python
import jax
import jax.numpy as jnp
from jax import lax
from jax.experimental import pallas as pl
from jax.experimental.pallas import tpu as pltpu
from jax.sharding import PartitionSpec as P

MESH = pl.DeviceIdType.MESH
F32 = jnp.float32
BF16 = jnp.bfloat16

ROWS = 1536
WIDE = 256
SUB = 3
SUBW = ROWS // SUB
BLOCKS = 2 * SUB
PIECE = 32
CROWS = PIECE + 16
AHEAD = 3
NN = (((1,), (0,)), ((), ()))
NT = (((1,), (1,)), ((), ()))
TN = (((0,), (0,)), ((), ()))


def dot(a, b, dims, precision=None):
    return lax.dot_general(a, b, dims, preferred_element_type=F32, precision=precision)


def exchange_kernel(
    a_ref, v_ref, a_out, x_ref, y_ref,
    vt, q_send, q_own, sib_in, x_send, x_in, z_send, z_in, zz_in, xx_send, xx_in,
    prt, c_send, c_col, c_full, c_sib,
    a_sem, s_send, s_recv,
):
    row = lax.axis_index("row")
    col = lax.axis_index("col")
    core = row % 2
    big = row // 2
    z = big % 4
    xl = big // 4
    yy = col % 4
    xh = col // 4

    sibling = (big * 2 + 1 - core, col)
    x_peer = (((1 - xl) * 4 + z) * 2 + core, col)
    z_peers = [((xl * 4 + (z + j) % 4) * 2 + core, col) for j in range(1, 4)]
    h_peer = (row, (1 - xh) * 4 + yy)
    y_peers = [(row, xh * 4 + (yy + j) % 4) for j in range(1, 4)]
    row_peers = [x_peer] + z_peers + [(((1 - xl) * 4 + (z + j) % 4) * 2 + core, col) for j in range(1, 4)]
    col_peers = [h_peer] + y_peers + [(row, (1 - xh) * 4 + (yy + j) % 4) for j in range(1, 4)]
    mirror = (col * 2 + core, big)
    on_diagonal = big == col
    off_diagonal = jnp.logical_not(on_diagonal)

    used = [0]
    sent = []

    def copy(src, dst, to):
        i = used[0]
        used[0] += 1
        return pltpu.make_async_remote_copy(
            src_ref=src, dst_ref=dst, send_sem=s_send.at[i], recv_sem=s_recv.at[i],
            device_id=to, device_id_type=MESH,
        )

    def send(src, dst, to):
        c = copy(src, dst, to)
        c.start()
        sent.append(c)
        return c

    loads = []
    for i in range(BLOCKS):
        b = (1 - core if i % 2 == 0 else core) * SUB + i // 2
        start = pl.multiple_of(b * SUBW, 128)
        loads.append((b, pltpu.make_async_copy(a_ref.at[:, pl.ds(start, SUBW)], a_out.at[b], a_sem.at[i])))
    for _, load in loads[:AHEAD]:
        load.start()

    barrier = pltpu.get_barrier_semaphore()
    for peer in [sibling] + row_peers + col_peers:
        pl.semaphore_signal(barrier, inc=1, device_id=peer, device_id_type=MESH)

    @pl.when(off_diagonal)
    def _():
        pl.semaphore_signal(barrier, inc=1, device_id=mirror, device_id_type=MESH)

    vt[:128, :] = v_ref[0].T
    vt[128:, :] = v_ref[1].T

    mine = pl.multiple_of(big * PIECE, PIECE)
    mine_v = pl.multiple_of(WIDE + big * PIECE, PIECE)
    mine_r = pl.multiple_of(col * PIECE, PIECE)
    half = pl.multiple_of(core * ROWS, ROWS)
    v_turn = copy(
        vt.at[pl.ds(mine_r, PIECE)],
        y_ref.at[pl.ds(pl.multiple_of(WIDE + col * PIECE, PIECE), PIECE), pl.ds(half, ROWS)],
        mirror,
    )

    sib = []
    for i, (b, load) in enumerate(loads):
        load.wait()
        if i + AHEAD < BLOCKS:
            loads[i + AHEAD][1].start()
        part = dot(vt[...], a_out[b], NN).reshape(2, 4, PIECE, SUBW)
        if i == 0:

            @pl.when(on_diagonal)
            def _():
                pl.semaphore_wait(barrier, 15)
                y_ref[pl.ds(mine_v, PIECE), pl.ds(half, ROWS)] = vt[pl.ds(mine_r, PIECE), :]

            @pl.when(off_diagonal)
            def _():
                pl.semaphore_wait(barrier, 16)
                v_turn.start()

        if i % 2 == 0:
            q_send[i // 2] = part.astype(BF16)
            sib.append(send(q_send.at[i // 2], sib_in.at[i // 2], sibling))
        else:
            q_own[i // 2] = part

    sib[0].wait_recv()
    q_own[0] = q_own[0] + sib_in[0].astype(F32)
    q_send_z = z_send.at[0]
    q_send_z[...] = q_own[0].astype(BF16)
    zz = [send(q_send_z.at[:, (z + j) % 4], zz_in.at[j - 1], z_peers[j - 1]) for j in range(1, 4)]
    xs = [None]
    for s in range(1, SUB):
        sib[s].wait_recv()
        x_send[s - 1] = (q_own[s, 1 - xl] + sib_in[s, 1 - xl].astype(F32)).astype(BF16)
        xs.append(send(x_send.at[s - 1], x_in.at[s - 1], x_peer))
        q_own[s, xl] = q_own[s, xl] + sib_in[s, xl].astype(F32)

    @pl.when(off_diagonal)
    def _():
        v_turn.wait()

    v_place = y_ref.at[pl.ds(mine_v, PIECE), pl.ds(half, ROWS)]
    v_x = send(v_place, v_place, x_peer)
    v_wait = [send(v_place, v_place, p) for p in z_peers]

    for c in zz:
        c.wait_recv()
    total = q_own[0, :, z]
    for j in range(3):
        total = total + zz_in[j].astype(F32)
    q_own[0, :, z] = total
    xx_send[...] = q_own[0, 1 - xl, z].astype(BF16)
    xx = send(xx_send, xx_in, x_peer)

    zs = [None]
    for s in range(1, SUB):
        xs[s].wait_recv()
        total = q_own[s, xl] + x_in[s - 1].astype(F32)
        q_own[s, xl] = total
        z_send[s, 0] = total.astype(BF16)
        zs.append(
            [send(z_send.at[s, 0, (z + j) % 4], z_in.at[s - 1, j - 1], z_peers[j - 1]) for j in range(1, 4)]
        )

    v_x.wait_recv()
    other_v = pl.multiple_of(WIDE + ((1 - xl) * 4 + z) * PIECE, PIECE)
    v_place2 = y_ref.at[pl.ds(other_v, PIECE), pl.ds(half, ROWS)]
    v_wait += [send(v_place2, v_place2, p) for p in z_peers]

    turns = []
    p_x = []
    p_wait = [[] for _ in range(SUB)]
    for s in range(SUB):
        if s == 0:
            xx.wait_recv()
            total = q_own[0, xl, z] + xx_in[...].astype(F32)
        else:
            total = q_own[s, xl, z]
            for j in range(3):
                zs[s][j].wait_recv()
                total = total + z_in[s - 1, j].astype(F32)
        columns = pl.ds(pl.multiple_of(core * ROWS + s * SUBW, 128), SUBW)
        place = y_ref.at[pl.ds(mine, PIECE), columns]
        place[...] = total.astype(BF16)
        turn = copy(place, prt.at[pl.ds(mine, PIECE), pl.ds(s * SUBW, SUBW)], mirror)
        turns.append(turn)

        @pl.when(off_diagonal)
        def _():
            turn.start()

        @pl.when(on_diagonal)
        def _():
            prt[pl.ds(mine, PIECE), pl.ds(s * SUBW, SUBW)] = place[...]

        p_x.append(send(place, place, x_peer))
        p_wait[s] += [send(place, place, p) for p in z_peers]

    for c in v_wait:
        c.wait_recv()
    v_place = y_ref.at[pl.ds(WIDE, WIDE), pl.ds(half, ROWS)]
    v_share = send(v_place, v_place, sibling)
    v_half = v_place[...]
    c_send[0, :PIECE, :] = dot(y_ref[pl.ds(mine, PIECE), pl.ds(half, ROWS)], v_half, NT)
    c_send[0, PIECE:, :] = dot(
        y_ref[pl.ds(pl.multiple_of(WIDE + big * 16, 16), 16), pl.ds(half, ROWS)], v_half, NT
    )
    c_full[16] = c_send[0].astype(BF16)
    cc = [send(c_full.at[16], c_col.at[j], p) for j, p in enumerate(col_peers)]

    r_x = []
    r_wait = [[] for _ in range(SUB)]
    for s in range(SUB):

        @pl.when(off_diagonal)
        def _():
            turns[s].wait()

        place = prt.at[pl.ds(mine_r, PIECE), pl.ds(s * SUBW, SUBW)]
        r_x.append(send(place, place, h_peer))
        r_wait[s] += [send(place, place, p) for p in y_peers]

    other_p = pl.multiple_of(((1 - xl) * 4 + z) * PIECE, PIECE)
    for s in range(SUB):
        p_x[s].wait_recv()
        place = y_ref.at[pl.ds(other_p, PIECE), pl.ds(pl.multiple_of(core * ROWS + s * SUBW, 128), SUBW)]
        p_wait[s] += [send(place, place, p) for p in z_peers]

    total = c_send[0]
    for j in range(7):
        cc[j].wait_recv()
        total = total + c_col[j].astype(F32)
    c_full[core * 8 + big] = total.astype(BF16)
    place = c_full.at[core * 8 + big]
    cr = [send(place, place, p) for p in row_peers]

    other_r = pl.multiple_of(((1 - xh) * 4 + yy) * PIECE, PIECE)
    for s in range(SUB):
        r_x[s].wait_recv()
        place = prt.at[pl.ds(other_r, PIECE), pl.ds(s * SUBW, SUBW)]
        r_wait[s] += [send(place, place, p) for p in y_peers]

    for c in cr:
        c.wait_recv()
    place = c_full.at[pl.ds(pl.multiple_of(core * 8, 8), 8)]
    c_share = send(place, c_sib, sibling)
    c_share.wait_recv()

    crows = [c_full[core * 8 + i].astype(F32) + c_sib[i].astype(F32) for i in range(8)]
    cpv = jnp.concatenate([m[:PIECE] for m in crows], axis=0)
    g01 = jnp.concatenate([m[PIECE:, 128:] for m in crows], axis=0)
    hi = lax.Precision.HIGHEST
    c00 = cpv[:128, :128]
    c01 = cpv[:128, 128:]
    c11 = cpv[128:, 128:]
    d = c01 - dot(c00, g01, NN, hi)
    curv = c11 - dot(c01, g01, TN, hi) - dot(g01, d, TN, hi)
    t2 = -jnp.concatenate(
        [jnp.concatenate([c00, d], axis=1), jnp.concatenate([d.T, curv], axis=1)], axis=0
    )
    t2b = t2.astype(BF16)
    g01b = g01.astype(BF16)

    p_share = []
    for s in range(SUB):
        for c in p_wait[s]:
            c.wait_recv()
        place = y_ref.at[pl.ds(0, WIDE), pl.ds(pl.multiple_of(core * ROWS + s * SUBW, 128), SUBW)]
        p_share.append(send(place, place, sibling))

    for s in range(SUB):
        rows = slice(s * SUBW, (s + 1) * SUBW)
        v0 = v_ref[0, rows]
        v1 = v_ref[1, rows]
        x_ref[rows, :128] = (v0.astype(F32) - dot(v1, g01b, NT)).astype(BF16)
        x_ref[rows, 128:256] = v1
        vt2 = dot(v0, t2b[:128], NN) + dot(v1, t2b[128:], NN)
        for c in r_wait[s]:
            c.wait_recv()
        p0 = prt[:128, rows].T
        p1 = prt[128:, rows].T
        x_ref[rows, 256:384] = (vt2[:, :128] + p0.astype(F32)).astype(BF16)
        x_ref[rows, 384:] = (vt2[:, 128:] + p1.astype(F32) - dot(p0, g01b, NN)).astype(BF16)

    v_share.wait_recv()
    for c in p_share:
        c.wait_recv()
    for c in sent:
        c.wait_send()


N_COPIES = 160


def exchange(matrix, panels):
    return pl.pallas_call(
        exchange_kernel,
        out_shape=(
            jax.ShapeDtypeStruct((BLOCKS, ROWS, SUBW), BF16),
            jax.ShapeDtypeStruct((ROWS, 2 * WIDE), BF16),
            jax.ShapeDtypeStruct((2 * WIDE, 2 * ROWS), BF16),
        ),
        in_specs=[pl.BlockSpec(memory_space=pl.ANY), pl.BlockSpec(memory_space=pltpu.VMEM)],
        out_specs=(pl.BlockSpec(memory_space=pltpu.VMEM),) * 3,
        scratch_shapes=[
            pltpu.VMEM((WIDE, ROWS), BF16),
            pltpu.VMEM((SUB, 2, 4, PIECE, SUBW), BF16),
            pltpu.VMEM((SUB, 2, 4, PIECE, SUBW), F32),
            pltpu.VMEM((SUB, 2, 4, PIECE, SUBW), BF16),
            pltpu.VMEM((SUB - 1, 4, PIECE, SUBW), BF16),
            pltpu.VMEM((SUB - 1, 4, PIECE, SUBW), BF16),
            pltpu.VMEM((SUB, 2, 4, PIECE, SUBW), BF16),
            pltpu.VMEM((SUB - 1, 3, PIECE, SUBW), BF16),
            pltpu.VMEM((3, 2, PIECE, SUBW), BF16),
            pltpu.VMEM((PIECE, SUBW), BF16),
            pltpu.VMEM((PIECE, SUBW), BF16),
            pltpu.VMEM((WIDE, ROWS), BF16),
            pltpu.VMEM((1, CROWS, WIDE), F32),
            pltpu.VMEM((7, CROWS, WIDE), BF16),
            pltpu.VMEM((17, CROWS, WIDE), BF16),
            pltpu.VMEM((8, CROWS, WIDE), BF16),
            pltpu.SemaphoreType.DMA((BLOCKS,)),
            pltpu.SemaphoreType.DMA((N_COPIES,)),
            pltpu.SemaphoreType.DMA((N_COPIES,)),
        ],
        compiler_params=pltpu.CompilerParams(
            collective_id=0, has_side_effects=True, vmem_limit_bytes=36 * 2**20
        ),
        name="exchange",
    )(matrix, panels)


def update_kernel(a_ref, x_ref, y_ref, o_ref, held, sems):
    copies = []
    for b in range(BLOCKS):
        columns = slice(b * SUBW, (b + 1) * SUBW)
        held[b] = (a_ref[b].astype(F32) - dot(x_ref[...], y_ref[:, columns], NN)).astype(BF16)
        copies.append(pltpu.make_async_copy(held.at[b], o_ref.at[:, pl.ds(b * SUBW, SUBW)], sems.at[b]))
        copies[b].start()
    for c in copies:
        c.wait()


def update(a, x, y):
    return pl.pallas_call(
        update_kernel,
        out_shape=jax.ShapeDtypeStruct((ROWS, 2 * ROWS), BF16),
        in_specs=[pl.BlockSpec(memory_space=pltpu.VMEM)] * 3,
        out_specs=pl.BlockSpec(memory_space=pl.ANY),
        scratch_shapes=[pltpu.VMEM((BLOCKS, ROWS, SUBW), BF16), pltpu.SemaphoreType.DMA((BLOCKS,))],
        compiler_params=pltpu.CompilerParams(vmem_limit_bytes=36 * 2**20),
        name="update",
    )(a, x, y)


def per_device(matrix, panels):
    return update(*exchange(matrix, panels))


def solution(mesh):
    return jax.shard_map(
        per_device,
        mesh=mesh,
        in_specs=(P("row", "col"), P(None, "row", None)),
        out_specs=P("row", "col"),
        check_vma=False,
    )
```

```python
import jax
import jax.numpy as jnp
from jax import lax
from jax.experimental import pallas as pl
from jax.experimental.pallas import tpu as pltpu
from jax.sharding import PartitionSpec as P

MESH = pl.DeviceIdType.MESH
F32 = jnp.float32
BF16 = jnp.bfloat16

ROWS = 1536
WIDE = 256
SUB = 3
SUBW = ROWS // SUB
BLOCKS = 2 * SUB
PIECE = 32
Z_FIRST = ()
AHEAD = 6
NN = (((1,), (0,)), ((), ()))
NT = (((1,), (1,)), ((), ()))


def dot(a, b, dims, precision=None):
    return lax.dot_general(a, b, dims, preferred_element_type=F32, precision=precision)


def exchange_kernel(
    a_ref, v_hbm, x_ref, y_ref, a_out,
    v_ref, vt, q_send, q_own, sib_in, x_send, x_in, z_send, z_in, zz_in, xx_send, xx_in,
    prt, g_send, g_in, g_full, c_send, c_row, c_full, c_sib,
    a_sem, s_send, s_recv,
):
    row = lax.axis_index("row")
    col = lax.axis_index("col")
    core = row % 2
    big = row // 2
    z = big % 4
    xl = big // 4
    yy = col % 4
    xh = col // 4

    sibling = (big * 2 + 1 - core, col)
    x_peer = (((1 - xl) * 4 + z) * 2 + core, col)
    z_peers = [((xl * 4 + (z + j) % 4) * 2 + core, col) for j in range(1, 4)]
    h_peer = (row, (1 - xh) * 4 + yy)
    y_peers = [(row, xh * 4 + (yy + j) % 4) for j in range(1, 4)]
    row_peers = [x_peer] + z_peers + [(((1 - xl) * 4 + (z + j) % 4) * 2 + core, col) for j in range(1, 4)]
    col_peers = [h_peer] + y_peers + [(row, (1 - xh) * 4 + (yy + j) % 4) for j in range(1, 4)]
    mirror = (col * 2 + core, big)
    on_diagonal = big == col
    off_diagonal = jnp.logical_not(on_diagonal)

    used = [0]
    sent = []

    def copy(src, dst, to):
        i = used[0]
        used[0] += 1
        return pltpu.make_async_remote_copy(
            src_ref=src, dst_ref=dst, send_sem=s_send.at[i], recv_sem=s_recv.at[i],
            device_id=to, device_id_type=MESH,
        )

    def send(src, dst, to):
        c = copy(src, dst, to)
        c.start()
        sent.append(c)
        return c

    panel_load = pltpu.make_async_copy(v_hbm, v_ref, a_sem.at[BLOCKS])
    panel_load.start()
    loads = []
    for i in range(BLOCKS):
        b = (1 - core if i % 2 == 0 else core) * SUB + i // 2
        start = pl.multiple_of(b * SUBW, 128)
        loads.append((b, pltpu.make_async_copy(a_ref.at[:, pl.ds(start, SUBW)], a_out.at[b], a_sem.at[i])))
    for _, load in loads[:AHEAD]:
        load.start()

    barrier = pltpu.get_barrier_semaphore()
    for peer in [sibling] + row_peers + col_peers:
        pl.semaphore_signal(barrier, inc=1, device_id=peer, device_id_type=MESH)

    @pl.when(off_diagonal)
    def _():
        pl.semaphore_signal(barrier, inc=1, device_id=mirror, device_id_type=MESH)

    panel_load.wait()
    vt[:128, :] = v_ref[0].T
    vt[128:, :] = v_ref[1].T
    g_send[0] = dot(vt[pl.ds(pl.multiple_of(col * 16, 16), 16), :], vt[128:, :], NT)

    mine = pl.multiple_of(big * PIECE, PIECE)
    mine_v = pl.multiple_of(WIDE + big * PIECE, PIECE)
    mine_r = pl.multiple_of(col * PIECE, PIECE)
    half = pl.multiple_of(core * ROWS, ROWS)

    def columns(s):
        return pl.ds(pl.multiple_of(core * ROWS + s * SUBW, 128), SUBW)

    v_turn = copy(
        vt.at[pl.ds(mine_r, PIECE)],
        y_ref.at[pl.ds(pl.multiple_of(WIDE + col * PIECE, PIECE), PIECE), pl.ds(half, ROWS)],
        mirror,
    )
    sib = []
    xs = [None] * SUB
    zs = [None] * SUB

    def reduce_first(s):
        sib[s].wait_recv()
        if s in Z_FIRST:
            total = q_own[s] + sib_in[s].astype(F32)
            q_own[s] = total
            z_send[s] = total.astype(BF16)
            zs[s] = [send(z_send.at[s, :, (z + j) % 4], zz_in.at[s, j - 1], z_peers[j - 1]) for j in range(1, 4)]
        else:
            x_send[s] = (q_own[s, 1 - xl] + sib_in[s, 1 - xl].astype(F32)).astype(BF16)
            xs[s] = send(x_send.at[s], x_in.at[s], x_peer)
            q_own[s, xl] = q_own[s, xl] + sib_in[s, xl].astype(F32)

    def reduce_second(s):
        if s in Z_FIRST:
            for c in zs[s]:
                c.wait_recv()
            total = q_own[s, :, z]
            for j in range(3):
                total = total + zz_in[s, j].astype(F32)
            q_own[s, :, z] = total
            xx_send[s] = q_own[s, 1 - xl, z].astype(BF16)
            xs[s] = send(xx_send.at[s], xx_in.at[s], x_peer)
        else:
            xs[s].wait_recv()
            total = q_own[s, xl] + x_in[s].astype(F32)
            q_own[s, xl] = total
            z_send[s, 0] = total.astype(BF16)
            zs[s] = [send(z_send.at[s, 0, (z + j) % 4], z_in.at[s, j - 1], z_peers[j - 1]) for j in range(1, 4)]

    turns = [None] * SUB
    p_x = [None] * SUB
    p_wait = [[] for _ in range(SUB)]

    def reduce_last(s):
        if s in Z_FIRST:
            xs[s].wait_recv()
            total = q_own[s, xl, z] + xx_in[s].astype(F32)
        else:
            total = q_own[s, xl, z]
            for j in range(3):
                zs[s][j].wait_recv()
                total = total + z_in[s, j].astype(F32)
        place = y_ref.at[pl.ds(mine, PIECE), columns(s)]
        place[...] = total.astype(BF16)
        turn = copy(place, prt.at[pl.ds(mine, PIECE), pl.ds(s * SUBW, SUBW)], mirror)
        turns[s] = turn

        @pl.when(off_diagonal)
        def _():
            turn.start()

        @pl.when(on_diagonal)
        def _():
            prt[pl.ds(mine, PIECE), pl.ds(s * SUBW, SUBW)] = place[...]

        p_x[s] = send(place, place, x_peer)
        p_wait[s] += [send(place, place, p) for p in z_peers]

    for i, (b, load) in enumerate(loads):
        load.wait()
        if i + AHEAD < BLOCKS:
            loads[i + AHEAD][1].start()
        part = dot(vt[...], a_out[b], NN).reshape(2, 4, PIECE, SUBW)
        if i % 2 == 0:
            q_send[i // 2] = part.astype(BF16)
        else:
            q_own[i // 2] = part
        if i == 1:

            @pl.when(on_diagonal)
            def _():
                pl.semaphore_wait(barrier, 15)
                y_ref[pl.ds(mine_v, PIECE), pl.ds(half, ROWS)] = vt[pl.ds(mine_r, PIECE), :]

            @pl.when(off_diagonal)
            def _():
                pl.semaphore_wait(barrier, 16)
                v_turn.start()

            sib.append(send(q_send.at[0], sib_in.at[0], sibling))
            g_sib = send(g_send.at[0], g_in.at[7], sibling)
        if i == 2 or i == 4:
            sib.append(send(q_send.at[i // 2], sib_in.at[i // 2], sibling))
        if i == 2:
            reduce_first(0)
        if i == 4:
            g_sib.wait_recv()
            g_send[1] = g_send[0] + g_in[7]
            gr = [send(g_send.at[1], g_in.at[j], p) for j, p in enumerate(row_peers)]
        if i == 4:
            reduce_first(1)
    reduce_first(2)

    @pl.when(off_diagonal)
    def _():
        v_turn.wait()

    v_place = y_ref.at[pl.ds(mine_v, PIECE), pl.ds(half, ROWS)]
    v_x = send(v_place, v_place, x_peer)
    v_wait = [send(v_place, v_place, p) for p in z_peers]
    total = g_send[1]
    for j in range(7):
        gr[j].wait_recv()
        total = total + g_in[j]
    place = g_full.at[pl.ds(pl.multiple_of(col * 16, 16), 16)]
    place[...] = total
    gc = [send(place, place, p) for p in col_peers]
    reduce_second(0)
    reduce_second(1)
    reduce_second(2)
    reduce_last(0)
    reduce_last(1)
    reduce_last(2)

    r_x = []
    r_wait = [[] for _ in range(SUB)]
    for s in range(SUB):

        @pl.when(off_diagonal)
        def _():
            turns[s].wait()

        place = prt.at[pl.ds(mine_r, PIECE), pl.ds(s * SUBW, SUBW)]
        r_x.append(send(place, place, h_peer))
        r_wait[s] += [send(place, place, p) for p in y_peers]
        part = dot(place[...], vt[:, s * SUBW:(s + 1) * SUBW], NT)
        if s == 0:
            c_send[...] = part
        else:
            c_send[...] = c_send[...] + part
    c_full[16] = c_send[...].astype(BF16)
    cr = [send(c_full.at[16], c_row.at[j], p) for j, p in enumerate(row_peers)]
    for c in v_wait:
        c.wait_recv()
    place = y_ref.at[pl.ds(pl.multiple_of(WIDE + xl * 128, 128), 128), pl.ds(half, ROWS)]
    v_share = [send(place, place, sibling)]

    other_p = pl.multiple_of(((1 - xl) * 4 + z) * PIECE, PIECE)
    for s in range(SUB):
        p_x[s].wait_recv()
        place = y_ref.at[pl.ds(other_p, PIECE), columns(s)]
        p_wait[s] += [send(place, place, p) for p in z_peers]

    total = c_send[...]
    for j in range(7):
        cr[j].wait_recv()
        total = total + c_row[j].astype(F32)
    place = c_full.at[core * 8 + col]
    place[...] = total.astype(BF16)
    cc = [send(place, place, p) for p in col_peers]

    other_r = pl.multiple_of(((1 - xh) * 4 + yy) * PIECE, PIECE)
    for s in range(SUB):
        r_x[s].wait_recv()
        place = prt.at[pl.ds(other_r, PIECE), pl.ds(s * SUBW, SUBW)]
        r_wait[s] += [send(place, place, p) for p in y_peers]

    v_x.wait_recv()
    place = y_ref.at[
        pl.ds(pl.multiple_of(WIDE + ((1 - xl) * 4 + z) * PIECE, PIECE), PIECE), pl.ds(half, ROWS)
    ]
    v_wait = [send(place, place, p) for p in z_peers]

    for c in gc:
        c.wait_recv()
    g01 = g_full[...]
    g01b = g01.astype(BF16)
    for s in range(SUB):
        rows = slice(s * SUBW, (s + 1) * SUBW)
        v1 = v_ref[1, rows]
        x_ref[rows, :128] = (v_ref[0, rows].astype(F32) - dot(v1, g01b, NT)).astype(BF16)
        x_ref[rows, 128:256] = v1

    for c in cc:
        c.wait_recv()
    place = c_full.at[pl.ds(pl.multiple_of(core * 8, 8), 8)]
    c_share = send(place, c_sib, sibling)
    c_share.wait_recv()

    cpv = jnp.concatenate([c_full[core * 8 + i].astype(F32) + c_sib[i].astype(F32) for i in range(8)], axis=0)
    cs = jnp.concatenate(
        [cpv[:, :128], cpv[:, 128:] - dot(cpv[:, :128], g01, NN, lax.Precision.HIGHEST)], axis=1
    ).astype(BF16)

    p_share = []
    for s in range(SUB):
        for c in p_wait[s]:
            c.wait_recv()
        place = y_ref.at[pl.ds(0, WIDE), columns(s)]
        p_share.append(send(place, place, sibling))

    for c in v_wait:
        c.wait_recv()
    place = y_ref.at[pl.ds(pl.multiple_of(WIDE + (1 - xl) * 128, 128), 128), pl.ds(half, ROWS)]
    v_share.append(send(place, place, sibling))

    for s in range(SUB):
        rows = slice(s * SUBW, (s + 1) * SUBW)
        vc = dot(x_ref[rows, :256], cs, NN)
        for c in r_wait[s]:
            c.wait_recv()
        p0 = prt[:128, rows].T
        p1 = prt[128:, rows].T
        x_ref[rows, 256:384] = (p0.astype(F32) - vc[:, :128]).astype(BF16)
        x_ref[rows, 384:] = (p1.astype(F32) - dot(p0, g01b, NN) - vc[:, 128:]).astype(BF16)

    for c in v_share + p_share:
        c.wait_recv()
    for c in sent:
        c.wait_send()


N_COPIES = 128


def exchange(matrix, panels):
    return pl.pallas_call(
        exchange_kernel,
        out_shape=(
            jax.ShapeDtypeStruct((ROWS, 2 * WIDE), BF16),
            jax.ShapeDtypeStruct((2 * WIDE, 2 * ROWS), BF16),
            jax.ShapeDtypeStruct((BLOCKS, ROWS, SUBW), BF16),
        ),
        in_specs=[pl.BlockSpec(memory_space=pltpu.HBM)] * 2,
        out_specs=(pl.BlockSpec(memory_space=pltpu.VMEM),) * 3,
        scratch_shapes=[
            pltpu.VMEM((2, ROWS, WIDE // 2), BF16),
            pltpu.VMEM((WIDE, ROWS), BF16),
            pltpu.VMEM((SUB, 2, 4, PIECE, SUBW), BF16),
            pltpu.VMEM((SUB, 2, 4, PIECE, SUBW), F32),
            pltpu.VMEM((SUB, 2, 4, PIECE, SUBW), BF16),
            pltpu.VMEM((SUB, 4, PIECE, SUBW), BF16),
            pltpu.VMEM((SUB, 4, PIECE, SUBW), BF16),
            pltpu.VMEM((SUB, 2, 4, PIECE, SUBW), BF16),
            pltpu.VMEM((SUB, 3, PIECE, SUBW), BF16),
            pltpu.VMEM((SUB, 3, 2, PIECE, SUBW), BF16),
            pltpu.VMEM((SUB, PIECE, SUBW), BF16),
            pltpu.VMEM((SUB, PIECE, SUBW), BF16),
            pltpu.VMEM((WIDE, ROWS), BF16),
            pltpu.VMEM((2, 16, 128), F32),
            pltpu.VMEM((8, 16, 128), F32),
            pltpu.VMEM((128, 128), F32),
            pltpu.VMEM((PIECE, WIDE), F32),
            pltpu.VMEM((7, PIECE, WIDE), BF16),
            pltpu.VMEM((17, PIECE, WIDE), BF16),
            pltpu.VMEM((8, PIECE, WIDE), BF16),
            pltpu.SemaphoreType.DMA((BLOCKS + 1,)),
            pltpu.SemaphoreType.DMA((N_COPIES,)),
            pltpu.SemaphoreType.DMA((N_COPIES,)),
        ],
        compiler_params=pltpu.CompilerParams(
            collective_id=0, has_side_effects=True, vmem_limit_bytes=36 * 2**20
        ),
        name="exchange",
    )(matrix, panels)


def update_kernel(x_ref, y_ref, a_ref, o_ref, held, sems):
    copies = []
    parts = [(b, 0, ROWS) for b in range(BLOCKS - 1)] + [(BLOCKS - 1, i * ROWS // 3, ROWS // 3) for i in range(3)]
    for i, (b, start, count) in enumerate(parts):
        columns = slice(b * SUBW, (b + 1) * SUBW)
        rows = slice(start, start + count)
        held[b, rows] = (a_ref[b, rows].astype(F32) - dot(x_ref[rows], y_ref[:, columns], NN)).astype(BF16)
        copies.append(
            pltpu.make_async_copy(
                held.at[b, pl.ds(start, count)], o_ref.at[pl.ds(start, count), pl.ds(b * SUBW, SUBW)], sems.at[i]
            )
        )
        copies[i].start()
    for c in copies:
        c.wait()


def update(x, y, a):
    return pl.pallas_call(
        update_kernel,
        out_shape=jax.ShapeDtypeStruct((ROWS, 2 * ROWS), BF16),
        in_specs=[pl.BlockSpec(memory_space=pltpu.VMEM)] * 3,
        out_specs=pl.BlockSpec(memory_space=pl.ANY),
        scratch_shapes=[pltpu.VMEM((BLOCKS, ROWS, SUBW), BF16), pltpu.SemaphoreType.DMA((BLOCKS + 2,))],
        compiler_params=pltpu.CompilerParams(vmem_limit_bytes=36 * 2**20),
        name="update",
    )(x, y, a)


def per_device(matrix, panels):
    panels = pltpu.with_memory_space_constraint(panels, pltpu.HBM)
    return update(*exchange(matrix, panels))


def solution(mesh):
    return jax.shard_map(
        per_device,
        mesh=mesh,
        in_specs=(P("row", "col"), P(None, "row", None)),
        out_specs=P("row", "col"),
        check_vma=False,
    )
```

```python
import jax
import jax.numpy as jnp
from jax import lax
from jax.experimental import pallas as pl
from jax.experimental.pallas import tpu as pltpu
from jax.sharding import PartitionSpec as P

MESH = pl.DeviceIdType.MESH
F32 = jnp.float32
BF16 = jnp.bfloat16

ROWS = 1536
WIDE = 256
SUB = 3
SUBW = ROWS // SUB
BLOCKS = 2 * SUB
PIECE = 32
Z_FIRST = ()
AHEAD = 6
NN = (((1,), (0,)), ((), ()))
NT = (((1,), (1,)), ((), ()))


def dot(a, b, dims, precision=None):
    return lax.dot_general(a, b, dims, preferred_element_type=F32, precision=precision)


def exchange_kernel(
    a_ref, v_hbm, x_ref, y_ref, a_out,
    v_ref, vt, q_send, q_own, sib_in, x_send, x_in, z_send, z_in, zz_in, xx_send, xx_in,
    prt, g_send, g_in, g_full, c_send, c_row, c_full, c_sib,
    a_sem, s_send, s_recv,
):
    row = lax.axis_index("row")
    col = lax.axis_index("col")
    core = row % 2
    big = row // 2
    z = big % 4
    xl = big // 4
    yy = col % 4
    xh = col // 4

    sibling = (big * 2 + 1 - core, col)
    x_peer = (((1 - xl) * 4 + z) * 2 + core, col)
    z_peers = [((xl * 4 + (z + j) % 4) * 2 + core, col) for j in range(1, 4)]
    h_peer = (row, (1 - xh) * 4 + yy)
    y_peers = [(row, xh * 4 + (yy + j) % 4) for j in range(1, 4)]
    row_peers = [x_peer] + z_peers + [(((1 - xl) * 4 + (z + j) % 4) * 2 + core, col) for j in range(1, 4)]
    col_peers = [h_peer] + y_peers + [(row, (1 - xh) * 4 + (yy + j) % 4) for j in range(1, 4)]
    mirror = (col * 2 + core, big)
    on_diagonal = big == col
    off_diagonal = jnp.logical_not(on_diagonal)

    used = [0]
    sent = []

    def copy(src, dst, to):
        i = used[0]
        used[0] += 1
        return pltpu.make_async_remote_copy(
            src_ref=src, dst_ref=dst, send_sem=s_send.at[i], recv_sem=s_recv.at[i],
            device_id=to, device_id_type=MESH,
        )

    def send(src, dst, to):
        c = copy(src, dst, to)
        c.start()
        sent.append(c)
        return c

    panel_load = pltpu.make_async_copy(v_hbm, v_ref, a_sem.at[BLOCKS])
    panel_load.start()
    loads = []
    for i in range(BLOCKS):
        b = (1 - core if i % 2 == 0 else core) * SUB + i // 2
        start = pl.multiple_of(b * SUBW, 128)
        loads.append((b, pltpu.make_async_copy(a_ref.at[:, pl.ds(start, SUBW)], a_out.at[b], a_sem.at[i])))
    for _, load in loads[:AHEAD]:
        load.start()

    barrier = pltpu.get_barrier_semaphore()
    for peer in [sibling] + row_peers + col_peers:
        pl.semaphore_signal(barrier, inc=1, device_id=peer, device_id_type=MESH)

    @pl.when(off_diagonal)
    def _():
        pl.semaphore_signal(barrier, inc=1, device_id=mirror, device_id_type=MESH)

    panel_load.wait()
    vt[:128, :] = v_ref[0].T
    vt[128:, :] = v_ref[1].T
    g_send[0] = dot(vt[pl.ds(pl.multiple_of(col * 16, 16), 16), :], vt[128:, :], NT)

    mine = pl.multiple_of(big * PIECE, PIECE)
    mine_v = pl.multiple_of(WIDE + big * PIECE, PIECE)
    mine_r = pl.multiple_of(col * PIECE, PIECE)
    half = pl.multiple_of(core * ROWS, ROWS)

    def columns(s):
        return pl.ds(pl.multiple_of(core * ROWS + s * SUBW, 128), SUBW)

    v_turn = copy(
        vt.at[pl.ds(mine_r, PIECE)],
        y_ref.at[pl.ds(pl.multiple_of(WIDE + col * PIECE, PIECE), PIECE), pl.ds(half, ROWS)],
        mirror,
    )
    sib = []
    xs = [None] * SUB
    zs = [None] * SUB

    def reduce_first(s):
        sib[s].wait_recv()
        if s in Z_FIRST:
            total = q_own[s] + sib_in[s].astype(F32)
            q_own[s] = total
            z_send[s] = total.astype(BF16)
            zs[s] = [send(z_send.at[s, :, (z + j) % 4], zz_in.at[s, j - 1], z_peers[j - 1]) for j in range(1, 4)]
        else:
            x_send[s] = (q_own[s, 1 - xl] + sib_in[s, 1 - xl].astype(F32)).astype(BF16)
            xs[s] = send(x_send.at[s], x_in.at[s], x_peer)
            q_own[s, xl] = q_own[s, xl] + sib_in[s, xl].astype(F32)

    def reduce_second(s):
        if s in Z_FIRST:
            for c in zs[s]:
                c.wait_recv()
            total = q_own[s, :, z]
            for j in range(3):
                total = total + zz_in[s, j].astype(F32)
            q_own[s, :, z] = total
            xx_send[s] = q_own[s, 1 - xl, z].astype(BF16)
            xs[s] = send(xx_send.at[s], xx_in.at[s], x_peer)
        else:
            xs[s].wait_recv()
            total = q_own[s, xl] + x_in[s].astype(F32)
            q_own[s, xl] = total
            z_send[s, 0] = total.astype(BF16)
            zs[s] = [send(z_send.at[s, 0, (z + j) % 4], z_in.at[s, j - 1], z_peers[j - 1]) for j in range(1, 4)]

    turns = [None] * SUB
    p_x = [None] * SUB
    p_wait = [[] for _ in range(SUB)]

    def reduce_last(s):
        if s in Z_FIRST:
            xs[s].wait_recv()
            total = q_own[s, xl, z] + xx_in[s].astype(F32)
        else:
            total = q_own[s, xl, z]
            for j in range(3):
                zs[s][j].wait_recv()
                total = total + z_in[s, j].astype(F32)
        place = y_ref.at[pl.ds(mine, PIECE), columns(s)]
        place[...] = total.astype(BF16)
        turn = copy(place, prt.at[pl.ds(mine, PIECE), pl.ds(s * SUBW, SUBW)], mirror)
        turns[s] = turn

        @pl.when(off_diagonal)
        def _():
            turn.start()

        @pl.when(on_diagonal)
        def _():
            prt[pl.ds(mine, PIECE), pl.ds(s * SUBW, SUBW)] = place[...]

        p_x[s] = send(place, place, x_peer)
        p_wait[s] += [send(place, place, p) for p in z_peers]

    for i, (b, load) in enumerate(loads):
        load.wait()
        if i + AHEAD < BLOCKS:
            loads[i + AHEAD][1].start()
        part = dot(vt[...], a_out[b], NN).reshape(2, 4, PIECE, SUBW)
        if i % 2 == 0:
            q_send[i // 2] = part.astype(BF16)
        else:
            q_own[i // 2] = part
        if i == 1:

            @pl.when(on_diagonal)
            def _():
                pl.semaphore_wait(barrier, 15)
                y_ref[pl.ds(mine_v, PIECE), pl.ds(half, ROWS)] = vt[pl.ds(mine_r, PIECE), :]

            @pl.when(off_diagonal)
            def _():
                pl.semaphore_wait(barrier, 16)
                v_turn.start()

            sib.append(send(q_send.at[0], sib_in.at[0], sibling))
            g_sib = send(g_send.at[0], g_in.at[7], sibling)
        if i == 2 or i == 4:
            sib.append(send(q_send.at[i // 2], sib_in.at[i // 2], sibling))
        if i == 2:
            reduce_first(0)
        if i == 4:
            g_sib.wait_recv()
            g_send[1] = g_send[0] + g_in[7]
            gr = [send(g_send.at[1], g_in.at[j], p) for j, p in enumerate(row_peers)]
        if i == 4:
            reduce_first(1)
    reduce_first(2)

    @pl.when(off_diagonal)
    def _():
        v_turn.wait()

    v_place = y_ref.at[pl.ds(mine_v, PIECE), pl.ds(half, ROWS)]
    v_x = send(v_place, v_place, x_peer)
    v_wait = [send(v_place, v_place, p) for p in z_peers]
    reduce_second(0)
    reduce_second(1)
    reduce_second(2)
    total = g_send[1]
    for j in range(7):
        gr[j].wait_recv()
        total = total + g_in[j]
    place = g_full.at[pl.ds(pl.multiple_of(col * 16, 16), 16)]
    place[...] = total
    gc = [send(place, place, p) for p in col_peers]
    reduce_last(0)
    reduce_last(1)
    reduce_last(2)

    r_x = []
    r_wait = [[] for _ in range(SUB)]
    for s in range(SUB):

        @pl.when(off_diagonal)
        def _():
            turns[s].wait()

        place = prt.at[pl.ds(mine_r, PIECE), pl.ds(s * SUBW, SUBW)]
        r_x.append(send(place, place, h_peer))
        r_wait[s] += [send(place, place, p) for p in y_peers]
        part = dot(place[...], vt[:, s * SUBW:(s + 1) * SUBW], NT)
        if s == 0:
            c_send[...] = part
        else:
            c_send[...] = c_send[...] + part
    c_full[16] = c_send[...].astype(BF16)
    cr = [send(c_full.at[16], c_row.at[j], p) for j, p in enumerate(row_peers)]
    for c in v_wait:
        c.wait_recv()
    place = y_ref.at[pl.ds(pl.multiple_of(WIDE + xl * 128, 128), 128), pl.ds(half, ROWS)]
    v_share = [send(place, place, sibling)]

    other_p = pl.multiple_of(((1 - xl) * 4 + z) * PIECE, PIECE)
    for s in range(SUB):
        p_x[s].wait_recv()
        place = y_ref.at[pl.ds(other_p, PIECE), columns(s)]
        p_wait[s] += [send(place, place, p) for p in z_peers]

    total = c_send[...]
    for j in range(7):
        cr[j].wait_recv()
        total = total + c_row[j].astype(F32)
    place = c_full.at[core * 8 + col]
    place[...] = total.astype(BF16)
    cc = [send(place, place, p) for p in col_peers]

    other_r = pl.multiple_of(((1 - xh) * 4 + yy) * PIECE, PIECE)
    for s in range(SUB):
        r_x[s].wait_recv()
        place = prt.at[pl.ds(other_r, PIECE), pl.ds(s * SUBW, SUBW)]
        r_wait[s] += [send(place, place, p) for p in y_peers]

    v_x.wait_recv()
    place = y_ref.at[
        pl.ds(pl.multiple_of(WIDE + ((1 - xl) * 4 + z) * PIECE, PIECE), PIECE), pl.ds(half, ROWS)
    ]
    v_wait = [send(place, place, p) for p in z_peers]

    for c in gc:
        c.wait_recv()
    g01b = g_full[...].astype(BF16)
    for s in range(SUB):
        rows = slice(s * SUBW, (s + 1) * SUBW)
        v1 = v_ref[1, rows]
        x_ref[rows, :128] = (v_ref[0, rows].astype(F32) - dot(v1, g01b, NT)).astype(BF16)
        x_ref[rows, 128:256] = v1

    for c in cc:
        c.wait_recv()
    place = c_full.at[pl.ds(pl.multiple_of(core * 8, 8), 8)]
    c_share = send(place, c_sib, sibling)
    c_share.wait_recv()

    curvature = jnp.concatenate(
        [c_full[core * 8 + i].astype(F32) + c_sib[i].astype(F32) for i in range(8)], axis=0
    ).astype(BF16)

    p_share = []
    for s in range(SUB):
        for c in p_wait[s]:
            c.wait_recv()
        place = y_ref.at[pl.ds(0, WIDE), columns(s)]
        p_share.append(send(place, place, sibling))


    for s in range(SUB):
        rows = slice(s * SUBW, (s + 1) * SUBW)
        vc = dot(x_ref[rows, :256], curvature, NN)
        for c in r_wait[s]:
            c.wait_recv()
        p0 = prt[:128, rows].T
        p1 = prt[128:, rows].T
        first = (p0.astype(F32) - vc[:, :128]).astype(BF16)
        x_ref[rows, 256:384] = first
        x_ref[rows, 384:] = (p1.astype(F32) - vc[:, 128:] - dot(first, g01b, NN)).astype(BF16)
        if s == 0:
            for c in v_wait:
                c.wait_recv()
            place = y_ref.at[pl.ds(pl.multiple_of(WIDE + (1 - xl) * 128, 128), 128), pl.ds(half, ROWS)]
            v_share.append(send(place, place, sibling))

    for c in v_share + p_share:
        c.wait_recv()
    for c in sent:
        c.wait_send()


N_COPIES = 128


def exchange(matrix, panels):
    return pl.pallas_call(
        exchange_kernel,
        out_shape=(
            jax.ShapeDtypeStruct((ROWS, 2 * WIDE), BF16),
            jax.ShapeDtypeStruct((2 * WIDE, 2 * ROWS), BF16),
            jax.ShapeDtypeStruct((BLOCKS, ROWS, SUBW), BF16),
        ),
        in_specs=[pl.BlockSpec(memory_space=pltpu.HBM)] * 2,
        out_specs=(pl.BlockSpec(memory_space=pltpu.VMEM),) * 3,
        scratch_shapes=[
            pltpu.VMEM((2, ROWS, WIDE // 2), BF16),
            pltpu.VMEM((WIDE, ROWS), BF16),
            pltpu.VMEM((SUB, 2, 4, PIECE, SUBW), BF16),
            pltpu.VMEM((SUB, 2, 4, PIECE, SUBW), F32),
            pltpu.VMEM((SUB, 2, 4, PIECE, SUBW), BF16),
            pltpu.VMEM((SUB, 4, PIECE, SUBW), BF16),
            pltpu.VMEM((SUB, 4, PIECE, SUBW), BF16),
            pltpu.VMEM((SUB, 2, 4, PIECE, SUBW), BF16),
            pltpu.VMEM((SUB, 3, PIECE, SUBW), BF16),
            pltpu.VMEM((SUB, 3, 2, PIECE, SUBW), BF16),
            pltpu.VMEM((SUB, PIECE, SUBW), BF16),
            pltpu.VMEM((SUB, PIECE, SUBW), BF16),
            pltpu.VMEM((WIDE, ROWS), BF16),
            pltpu.VMEM((2, 16, 128), F32),
            pltpu.VMEM((8, 16, 128), F32),
            pltpu.VMEM((128, 128), F32),
            pltpu.VMEM((PIECE, WIDE), F32),
            pltpu.VMEM((7, PIECE, WIDE), BF16),
            pltpu.VMEM((17, PIECE, WIDE), BF16),
            pltpu.VMEM((8, PIECE, WIDE), BF16),
            pltpu.SemaphoreType.DMA((BLOCKS + 1,)),
            pltpu.SemaphoreType.DMA((N_COPIES,)),
            pltpu.SemaphoreType.DMA((N_COPIES,)),
        ],
        compiler_params=pltpu.CompilerParams(
            collective_id=0, has_side_effects=True, vmem_limit_bytes=36 * 2**20
        ),
        name="exchange",
    )(matrix, panels)


def update_kernel(x_ref, y_ref, a_ref, o_ref, held, sems):
    copies = []
    parts = [(b, 0, ROWS) for b in range(BLOCKS - 1)] + [(BLOCKS - 1, i * ROWS // 3, ROWS // 3) for i in range(3)]
    for i, (b, start, count) in enumerate(parts):
        columns = slice(b * SUBW, (b + 1) * SUBW)
        rows = slice(start, start + count)
        held[b, rows] = (a_ref[b, rows].astype(F32) - dot(x_ref[rows], y_ref[:, columns], NN)).astype(BF16)
        copies.append(
            pltpu.make_async_copy(
                held.at[b, pl.ds(start, count)], o_ref.at[pl.ds(start, count), pl.ds(b * SUBW, SUBW)], sems.at[i]
            )
        )
        copies[i].start()
    for c in copies:
        c.wait()


def update(x, y, a):
    return pl.pallas_call(
        update_kernel,
        out_shape=jax.ShapeDtypeStruct((ROWS, 2 * ROWS), BF16),
        in_specs=[pl.BlockSpec(memory_space=pltpu.VMEM)] * 3,
        out_specs=pl.BlockSpec(memory_space=pl.ANY),
        scratch_shapes=[pltpu.VMEM((BLOCKS, ROWS, SUBW), BF16), pltpu.SemaphoreType.DMA((BLOCKS + 2,))],
        compiler_params=pltpu.CompilerParams(vmem_limit_bytes=36 * 2**20),
        name="update",
    )(x, y, a)


def per_device(matrix, panels):
    panels = pltpu.with_memory_space_constraint(panels, pltpu.HBM)
    return update(*exchange(matrix, panels))


def solution(mesh):
    return jax.shard_map(
        per_device,
        mesh=mesh,
        in_specs=(P("row", "col"), P(None, "row", None)),
        out_specs=P("row", "col"),
        check_vma=False,
    )
```
